256 devices in a mesh: ctx: 64 (over z, x, core), tp: 4 (over y).
Axes of the slice: x: 4, y: 4, z: 8, core: 2. Of those that a mesh axis runs over, the one named last changes fastest.
Arguments:
- queries: bfloat16 [8192, 4096], P('ctx', 'tp'), may hold values from -80 to 80
- keys: bfloat16 [8192, 512], P('ctx', 'tp'), may hold values from -4 to 4
- values: bfloat16 [8192, 512], P('ctx', 'tp'), may hold values from -16 to 16
- segment_ids: int32 [8192], P('ctx'), may hold values from 0 to 15, never falling along the last dimension, each value on 1 to 4224 neighbouring positions
- out_weight: bfloat16 [4096, 4096], P('tp'), may hold values from -0.09375 to 0.09375
Outputs:
- mixed: bfloat16 [8192, 4096], P('ctx', 'tp')
The draws below stay inside these ranges and needn't reach their ends.
All inputs are finite; a program needn't handle non-finite values.
Results may differ from the reference program's by a relative error of at most 0.015.
Values may be sent and summed in bfloat16 or wider, within the bound.
No kernel may reach another device: no remote copies, remote signals or barrier semaphores. Data moves between devices by JAX's collectives and lax.ppermute only.
A program may use at most 128 MiB of HBM per device.

```python
import math
import jax
import jax.numpy as jnp
import numpy as np
from jax import lax

HEAD_DIM = 128
HEADS = 32
KV_HEADS = 4
D = 4096
T_DEV = 128
SEQ = 8192
DOCS = 16
DOC_MOST = 4224


def common_keys(key):
    base = jnp.clip(jax.random.normal(jax.random.fold_in(key, 11), (SEQ, KV_HEADS * HEAD_DIM), jnp.float32), -4.0, 4.0)
    picked = jax.random.bernoulli(jax.random.fold_in(key, 12), 1.0 / 64.0, (SEQ,)).astype(jnp.float32)
    moved = base
    return (jnp.clip(moved, -4.0, 4.0), picked)


def draw_keys(key, part):
    keys_all, picked = common_keys(key)
    return keys_all.astype(jnp.bfloat16)


def draw_queries(key, part):
    blend = 0.0
    keys_all, picked = common_keys(key)
    key = jax.random.fold_in(key, 5)
    drawn = jnp.clip(1.5 * jax.random.normal(key, (SEQ, HEADS * HEAD_DIM), jnp.float32), -6.0, 6.0)
    select = blend * picked
    mixed = drawn * (1.0 - select[:, None])
    return mixed.astype(jnp.bfloat16)


def level_of(stream_key, extent, cuts, least, top_value):
    loudness, own = 1.0, jax.random.fold_in(stream_key, 6)
    for dim, shards_of in cuts:
        steps = jnp.exp(jax.random.uniform(jax.random.fold_in(own, dim), (shards_of,), jnp.float32, least / len(cuts), top_value / len(cuts)))
        loudness = loudness * jnp.repeat(steps, extent[dim] // shards_of).reshape([-1 if axis == dim else 1 for axis in range(len(extent))])
    return loudness


def length_profile(count, total, most, lean):
    loads = [(1 << 20) // math.isqrt(grade ** lean) + 1 for grade in range(2, count + 1)]
    surplus, given = total - most - (count - 1), [1] * (count - 1)
    while surplus > 0:
        movable = [i for i in range(count - 1) if given[i] < most]
        pool, remaining = sum([loads[i] for i in movable]), surplus
        for i in movable:
            more = min(most - given[i], max(1, remaining * loads[i] // pool), surplus)
            given[i] = given[i] + more
            surplus = surplus - more
    return np.array([most] + given)


def uneven(key, number_of, total, bound, slope):
    if number_of == 2:
        one = jax.random.randint(key, (), max(1, total - bound), min(bound, total - 1) + 1)
        return jnp.stack([one, total - one])
    tallies = jnp.asarray(length_profile(number_of, total, bound, slope), jnp.int32)
    couples = (number_of - 1) // 2
    donor, receiver = tallies[1:1 + 2 * couples:2], tallies[2:2 + 2 * couples:2]
    slack = jnp.minimum(donor - 1, bound - receiver)
    passed = jax.random.randint(jax.random.fold_in(key, 1), (couples,), 0, 1 << 20) % (slack + 1)
    tallies = tallies.at[1:1 + 2 * couples:2].set(donor - passed).at[2:2 + 2 * couples:2].set(receiver + passed)
    return tallies[jax.random.permutation(jax.random.fold_in(key, 2), number_of)]


def gaussian(key, extent, deviation, most, cuts=(), held_as=jnp.bfloat16):
    loudness = level_of(key, extent, cuts, -0.22, 0.18) if cuts else 1.0
    entries = jax.random.normal(key, extent, jnp.float32) * deviation * loudness
    return jnp.minimum(jnp.maximum(entries, -most), most).astype(held_as)


def setup_inputs(seed: int = 0) -> dict:
    key_list = jax.random.split(jax.random.key(seed), 6)
    queries = draw_queries(jax.random.fold_in(key_list[5], 71), 0)
    keys = draw_keys(jax.random.fold_in(key_list[5], 71), 0)
    values = gaussian(key_list[2], (SEQ, KV_HEADS * HEAD_DIM), 4.0, 16.0, ((0, 64), (1, 4)))
    segment_ids = jnp.searchsorted(jnp.cumsum(uneven(key_list[3], DOCS, SEQ, DOC_MOST, 1)), jnp.arange(SEQ), side="right").astype(jnp.int32)
    out_weight = gaussian(key_list[4], (HEADS * HEAD_DIM, D), (HEADS * HEAD_DIM) ** -0.5, 0.09375, ((0, 4),))
    return dict(queries=queries, keys=keys, values=values, segment_ids=segment_ids, out_weight=out_weight)


def reference(queries, keys, values, segment_ids, out_weight):
    seq = queries.shape[0]
    group = HEADS // KV_HEADS
    block = 2 * T_DEV
    scale = HEAD_DIM ** -0.5
    query_blocks = queries.astype(jnp.float32).reshape(seq // block, block, KV_HEADS, group, HEAD_DIM)
    key_all = keys.astype(jnp.float32).reshape(seq, KV_HEADS, HEAD_DIM)
    value_all = values.astype(jnp.float32).reshape(seq, KV_HEADS, HEAD_DIM)
    positions = jnp.arange(seq, dtype=jnp.int32)
    query_pos = positions.reshape(seq // block, block)
    query_seg = segment_ids.reshape(seq // block, block)

    def one_block(args):
        query_block, pos_block, seg_block = args
        allowed = (positions[None, :] <= pos_block[:, None]) & (segment_ids[None, :] == seg_block[:, None])

        def one_head(head):
            query_head = query_block[:, head]
            scores = jnp.einsum('rgd,pd->grp', query_head, key_all[:, head]) * scale
            scores = jnp.where(allowed[None], scores, -1e30)
            largest = jnp.max(scores, axis=-1, keepdims=True)
            weight = jnp.exp(scores - largest) * allowed[None]
            total = jnp.sum(weight, axis=-1)
            rounded = lax.optimization_barrier(weight.astype(jnp.bfloat16)).astype(jnp.float32)
            summed = jnp.einsum('grp,pd->grd', rounded, value_all[:, head])
            return summed / total[..., None]

        result = lax.map(one_head, jnp.arange(KV_HEADS, dtype=jnp.int32))
        return result.transpose(2, 0, 1, 3).reshape(block, HEADS * HEAD_DIM)

    attention = lax.map(one_block, (query_blocks, query_pos, query_seg))
    attention = attention.reshape(seq, HEADS * HEAD_DIM).astype(jnp.bfloat16)
    return jnp.dot(attention, out_weight, preferred_element_type=jnp.float32).astype(jnp.bfloat16)
```

```python
import functools

import jax
import jax.numpy as jnp
from jax import lax
from jax.experimental import pallas as pl
from jax.experimental.pallas import tpu as pltpu
from jax.sharding import PartitionSpec as P

HEAD_DIM = 128
ROWS = 272
LOG2E = 1.4426950408889634
NEG = -1e30


def ctx_pairs(size, target):
    pairs = [(i, target(i)) for i in range(size)]
    return [(i, k) for i, k in pairs if k is not None and 0 <= k < size]


def shift_z(size, planes):
    return ctx_pairs(size, lambda i: i + 8 * planes)


def shift_x(size, steps):
    return ctx_pairs(size, lambda i: i // 8 * 8 + (i + 2 * steps) % 8)


def swap_core(size):
    return ctx_pairs(size, lambda i: i ^ 1)


def heads_of(q_ref):
    tokens, width = q_ref.shape
    return jnp.concatenate(
        [q_ref[:, h * HEAD_DIM : (h + 1) * HEAD_DIM] for h in range(width // HEAD_DIM)], 0
    )


def column(row):
    return jnp.transpose(jnp.broadcast_to(row, (128, 128)))


def absorb(q, state, keys, values, allowed, scale):
    m, acc = state
    n = keys.shape[0]
    s = lax.dot_general(q, keys, (((1,), (1,)), ((), ())), preferred_element_type=jnp.float32)
    s = jnp.where(allowed[None], s.reshape(-1, 128, n), NEG).reshape(-1, n)
    top = jnp.max(s, axis=1, keepdims=True)
    new_m = top if m is None else jnp.maximum(m, top)
    weight = jnp.exp2((s - new_m) * scale).astype(jnp.bfloat16)
    extended = jnp.concatenate([values, jnp.ones_like(values)], 1)
    part = jnp.dot(weight, extended, preferred_element_type=jnp.float32)
    if m is not None:
        part = acc * jnp.exp2((m - new_m) * scale) + part
    return new_m, part


def own_kernel(scale, q_ref, own_ref, m_ref, acc_ref):
    q = heads_of(q_ref)
    seg = own_ref[256:272, :].astype(jnp.float32)[0:1]
    later = lax.broadcasted_iota(jnp.int32, (128, 128), 1) > lax.broadcasted_iota(
        jnp.int32, (128, 128), 0
    )
    allowed = (column(seg) == seg) & ~later
    m, acc = absorb(
        q, (None, None), own_ref[0:128, :], own_ref[128:256, :], allowed, scale
    )
    m_ref[...] = jnp.broadcast_to(m, m_ref.shape)
    acc_ref[...] = acc


def group_kernel(scale, last, usable_ref, q_ref, own_ref, near_ref, far_ref, m_in, acc_in, *rest):
    if last:
        out_ref, m_ref, acc_ref = rest
    else:
        m_ref, acc_ref = rest
    _, n, _, _ = near_ref.shape
    m_ref[...] = m_in[...]
    acc_ref[...] = acc_in[...]
    q = heads_of(q_ref)
    own_seg = column(own_ref[256:272, :].astype(jnp.float32)[0:1])

    def step(x, carry):
        flags = [usable_ref[(side * 4 + x) * n + k] for k in range(n) for side in range(2)]
        some = functools.reduce(jnp.maximum, flags)

        @pl.when(some > 0)
        def _():
            blocks = [ref[x, k] for k in range(n) for ref in (near_ref, far_ref)]
            keys = jnp.concatenate([b[0:128] for b in blocks], 0)
            values = jnp.concatenate([b[128:256] for b in blocks], 0)
            allowed = jnp.concatenate(
                [
                    own_seg == jnp.where(flag > 0, b[256:272].astype(jnp.float32)[0:1], -1.0)
                    for b, flag in zip(blocks, flags)
                ],
                1,
            )
            m, acc = absorb(
                q, (m_ref[:, 0:1], acc_ref[...]), keys, values, allowed, scale
            )
            m_ref[...] = jnp.broadcast_to(m, m_ref.shape)
            acc_ref[...] = acc

        return carry

    lax.fori_loop(0, 4, step, 0)
    if last:
        for h in range(q_ref.shape[1] // HEAD_DIM):
            rows = slice(h * 128, (h + 1) * 128)
            out_ref[:, h * HEAD_DIM : (h + 1) * HEAD_DIM] = (
                acc_ref[rows, 0:128] / acc_ref[rows, 128:256]
            ).astype(out_ref.dtype)


VMEM = pl.BlockSpec(memory_space=pltpu.VMEM)
SMEM = pl.BlockSpec(memory_space=pltpu.SMEM)
PARAMS = pltpu.CompilerParams(vmem_limit_bytes=40 * 1024 * 1024)


def on_device(size, queries, keys, values, segment_ids, out_weight):
    tokens = queries.shape[0]
    rows = tokens * (queries.shape[1] // HEAD_DIM)
    scale = HEAD_DIM ** (-0.5) * LOG2E
    index = lax.axis_index("ctx")
    lane = lax.axis_index("tp")
    z, x, c = index // 8, index % 8 // 2, index % 2
    seg = (segment_ids + 1).astype(jnp.bfloat16)
    own = jnp.concatenate([keys, values, jnp.broadcast_to(seg[None], (16, tokens))], 0)

    def send(value, pairs):
        return lax.ppermute(value, "ctx", pairs)

    own1 = own[None]
    planes = [own1] + [send(own1, shift_z(size, k)) for k in (1, 2, 3, 4)]
    beyond = send(own, [(8 * k - 33, 8 * k) for k in range(5, size // 8)])

    def spread(part):
        sides = [send(part, shift_x(size, k)) for k in (2, 1, 3)]
        near = jnp.stack([part, *sides])
        return near, send(near, swap_core(size))

    def usable(plane_numbers):
        cells = []
        for side in range(2):
            for back in (0, 2, 1, 3):
                for k in plane_numbers:
                    g = 8 * (z - k) + 2 * ((x - back) % 4) + (c + side) % 2
                    cells.append((g >= 0) & (g < index))
        return jnp.stack(cells).astype(jnp.int32)

    state_shape = (
        jax.ShapeDtypeStruct((rows, 128), jnp.float32),
        jax.ShapeDtypeStruct((rows, 256), jnp.float32),
    )
    m, acc = pl.pallas_call(
        functools.partial(own_kernel, scale),
        out_shape=state_shape,
        in_specs=[VMEM] * 2,
        out_specs=(VMEM, VMEM),
        compiler_params=PARAMS,
        name="own",
    )(queries, own)

    group_a = spread(jnp.concatenate(planes[0:3], 0))
    group_b = spread(jnp.concatenate(planes[3:5], 0))

    m, acc = pl.pallas_call(
        functools.partial(group_kernel, scale, False),
        out_shape=state_shape,
        in_specs=[SMEM] + [VMEM] * 6,
        out_specs=(VMEM, VMEM),
        compiler_params=PARAMS,
        name="near",
    )(usable((0, 1, 2)), queries, own, *group_a, m, acc)

    beyond4 = jnp.concatenate([beyond[None, None], jnp.zeros((3, 1) + beyond.shape, beyond.dtype)])
    flag = jnp.zeros((8,), jnp.int32).at[0].set(((index % 8 == 0) & (z >= 5)).astype(jnp.int32))
    m, acc = pl.pallas_call(
        functools.partial(group_kernel, scale, False),
        out_shape=state_shape,
        in_specs=[SMEM] + [VMEM] * 6,
        out_specs=(VMEM, VMEM),
        compiler_params=PARAMS,
        name="beyond",
    )(flag, queries, own, beyond4, beyond4, m, acc)

    attention = pl.pallas_call(
        functools.partial(group_kernel, scale, True),
        out_shape=jax.ShapeDtypeStruct((tokens, queries.shape[1]), jnp.bfloat16),
        in_specs=[SMEM] + [VMEM] * 6,
        out_specs=VMEM,
        scratch_shapes=[pltpu.VMEM(s.shape, s.dtype) for s in state_shape],
        compiler_params=PARAMS,
        name="last",
    )(usable((3, 4)), queries, own, *group_b, m, acc)

    width = out_weight.shape[1] // 4
    partial_out = jnp.dot(attention, out_weight, preferred_element_type=jnp.float32)

    def share(k):
        return lax.dynamic_slice_in_dim(partial_out, (lane ^ k) * width, width, 1)

    total = share(0)
    for k in (2, 1, 3):
        got = lax.ppermute(share(k).astype(jnp.bfloat16), "tp", [(i, i ^ k) for i in range(4)])
        total = total + got.astype(jnp.float32)
    return total.astype(jnp.bfloat16)


def solution(mesh):
    placed = (P("ctx", "tp"), P("ctx", "tp"), P("ctx", "tp"), P("ctx"), P("tp", None))
    return jax.shard_map(
        functools.partial(on_device, mesh.shape["ctx"]),
        mesh=mesh,
        in_specs=placed,
        out_specs=P("ctx", "tp"),
        check_vma=False,
    )
```

```python
import functools

import jax
import jax.numpy as jnp
from jax import lax
from jax.experimental import pallas as pl
from jax.experimental.pallas import tpu as pltpu
from jax.sharding import PartitionSpec as P

HEAD_DIM = 128
LOG2E = 1.4426950408889634
SCALE = HEAD_DIM ** (-0.5) * LOG2E
NEG = -1e30
ACC_ROWS = 144

VMEM = pl.BlockSpec(memory_space=pltpu.VMEM)
SMEM = pl.BlockSpec(memory_space=pltpu.SMEM)
HBM = pl.BlockSpec(memory_space=pltpu.HBM)


def ctx_pairs(size, target):
    pairs = [(i, target(i)) for i in range(size)]
    return [(i, k) for i, k in pairs if 0 <= k < size]


def shift_z(size, planes):
    return ctx_pairs(size, lambda i: i + 8 * planes)


def shift_x(size, steps):
    return ctx_pairs(size, lambda i: i // 8 * 8 + (i + 2 * steps) % 8)


def swap_core(size):
    return ctx_pairs(size, lambda i: i ^ 1)


def params(mebibytes):
    return pltpu.CompilerParams(vmem_limit_bytes=mebibytes * 1024 * 1024)


def cost(blocks, rows, more=0):
    return pl.CostEstimate(
        flops=blocks * 128 * rows * 128 * 128 + more,
        bytes_accessed=blocks * 65536,
        transcendentals=blocks * 128 * rows,
    )


def seg_row(block):
    return block[256:272].astype(jnp.float32)[0:1]


def column(row):
    return jnp.transpose(jnp.broadcast_to(row, (128, 128)))


def absorb(q, m, acc, blocks, allowed):
    keys = jnp.concatenate([b[0:128] for b in blocks], 0)
    values = jnp.concatenate([b[128:256] for b in blocks], 1)
    s = lax.dot_general(keys, q, (((1,), (1,)), ((), ())), preferred_element_type=jnp.float32)
    allowed = jnp.concatenate(allowed, 0)
    s = jnp.concatenate(
        [jnp.where(allowed, s[:, h : h + 128], NEG) for h in range(0, s.shape[1], 128)], 1
    )
    top = jnp.max(s, axis=0, keepdims=True)
    new_m = top if m is None else jnp.maximum(m, top)
    weight = jnp.exp2((s - new_m) * SCALE).astype(jnp.bfloat16)
    ones = jnp.ones((ACC_ROWS - 128, values.shape[1]), values.dtype)
    part = jnp.dot(
        jnp.concatenate([values, ones], 0), weight, preferred_element_type=jnp.float32
    )
    if m is not None:
        part = acc * jnp.exp2((m - new_m) * SCALE) + part
    return new_m, part


def pack_kernel(k_ref, v_ref, seg_ref, out_ref, v_buf, seg_buf, sems):
    copies = [
        pltpu.make_async_copy(k_ref, out_ref.at[0, 0:128, :], sems.at[0]),
        pltpu.make_async_copy(v_ref, v_buf, sems.at[1]),
        pltpu.make_async_copy(seg_ref, seg_buf, sems.at[2]),
    ]
    for copy in copies:
        copy.start()
    for copy in copies:
        copy.wait()
    out_ref[0, 128:256, :] = jnp.transpose(v_buf[...].astype(jnp.float32)).astype(out_ref.dtype)
    seg = (seg_buf[...] + 1).astype(jnp.float32)
    out_ref[0, 256:272, :] = jnp.broadcast_to(seg, (16, 128)).astype(out_ref.dtype)


def own_kernel(q_ref, own_ref, m_ref, acc_ref, heads_ref):
    width = q_ref.shape[1]
    q = jnp.concatenate(
        [q_ref[:, h * HEAD_DIM : (h + 1) * HEAD_DIM] for h in range(width // HEAD_DIM)], 0
    )
    heads_ref[...] = q
    own = own_ref[0]
    seg = seg_row(own)
    later = lax.broadcasted_iota(jnp.int32, (128, 128), 0) > lax.broadcasted_iota(
        jnp.int32, (128, 128), 1
    )
    allowed = (column(seg) == seg) & ~later
    m, acc = absorb(q, None, None, [own], [allowed])
    m_ref[...] = jnp.broadcast_to(m, m_ref.shape)
    acc_ref[...] = acc


def gather_blocks(refs):
    return [ref[(*lead,)] for ref in refs for lead in _leads(ref.shape[:-2])]


def _leads(shape):
    if not shape:
        return [()]
    return [(i, *rest) for i in range(shape[0]) for rest in _leads(shape[1:])]


def run(q_ref, own_ref, m_in, acc_in, refs):
    blocks = gather_blocks(refs)
    seg = seg_row(own_ref[0])
    allowed = [column(seg_row(block)) == seg for block in blocks]
    return absorb(q_ref[...], m_in[0:1], acc_in[...], blocks, allowed)


def group_kernel(q_ref, own_ref, m_in, acc_in, *rest):
    *refs, m_ref, acc_ref = rest
    m, acc = run(q_ref, own_ref, m_in, acc_in, refs)
    m_ref[...] = jnp.broadcast_to(m, m_ref.shape)
    acc_ref[...] = acc


def last_kernel(lane_ref, q_ref, own_ref, m_in, acc_in, far_ref, beyond_ref, w_ref, *outs):
    own_out, *shares, att = outs
    _, acc = run(q_ref, own_ref, m_in, acc_in, [far_ref, beyond_ref])
    result = acc[0:128] / acc[128:129]
    for h in range(q_ref.shape[0] // att.shape[0]):
        part = slice(h * HEAD_DIM, (h + 1) * HEAD_DIM)
        att[:, part] = jnp.transpose(result[:, part]).astype(att.dtype)
    lane = lane_ref[0]
    width = own_out.shape[1]
    for k, ref in ((2, shares[0]), (1, shares[1]), (3, shares[2]), (0, own_out)):
        columns = pl.ds(pl.multiple_of((lane ^ k) * width, width), width)
        ref[...] = jnp.dot(
            att[...], w_ref[:, columns], preferred_element_type=jnp.float32
        ).astype(ref.dtype)


def on_device(size, queries, keys, values, segment_ids, out_weight):
    tokens = queries.shape[0]
    rows = tokens * (queries.shape[1] // HEAD_DIM)
    index = lax.axis_index("ctx")
    lane = lax.axis_index("tp")
    x, c = index % 8 // 2, index % 2

    def send(value, pairs):
        return lax.ppermute(value, "ctx", pairs)

    own = pl.pallas_call(
        pack_kernel,
        out_shape=jax.ShapeDtypeStruct((1, 272, 128), jnp.bfloat16),
        in_specs=[HBM] * 3,
        out_specs=VMEM,
        scratch_shapes=[
            pltpu.VMEM((128, 128), jnp.bfloat16),
            pltpu.VMEM((1, 128), jnp.int32),
            pltpu.SemaphoreType.DMA((3,)),
        ],
        compiler_params=params(2),
        name="pack",
    )(keys, values, segment_ids[None])

    state_shape = (
        jax.ShapeDtypeStruct((8, rows), jnp.float32),
        jax.ShapeDtypeStruct((ACC_ROWS, rows), jnp.float32),
    )

    def attend(name, state, blocks, operands):
        return pl.pallas_call(
            group_kernel,
            out_shape=state_shape,
            in_specs=[VMEM] * (4 + len(operands)),
            out_specs=(VMEM, VMEM),
            compiler_params=params(16),
            cost_estimate=cost(blocks, rows),
            name=name,
        )(heads, own, *state, *operands)

    p1 = send(own, shift_z(size, 1))
    p2 = send(own, shift_z(size, 2))
    *state, heads = pl.pallas_call(
        own_kernel,
        out_shape=(*state_shape, jax.ShapeDtypeStruct((rows, HEAD_DIM), queries.dtype)),
        in_specs=[VMEM] * 2,
        out_specs=(VMEM,) * 3,
        compiler_params=params(12),
        cost_estimate=cost(1, rows),
        name="own",
    )(queries, own)
    p12 = jnp.concatenate([p1, p2], 0)
    p12, state, heads = lax.optimization_barrier((p12, state, heads))

    near_a = [p12] + [send(p12, shift_x(size, k)) for k in (2, 1, 3)]
    p34 = send(p12, shift_z(size, 2))
    p34, near_a = lax.optimization_barrier((p34, near_a))

    def with_either(first):
        return jnp.concatenate([p34[0:1], jnp.where(first, own, p34[1:2])], 0)

    far_a = send(jnp.stack(near_a), swap_core(size))
    side_b = [send(with_either(x + k < 4), shift_x(size, k)) for k in (2, 1, 3)]
    beyond = send(p34[1:2], ctx_pairs(size, lambda i: i + 1))
    state = attend("near_a", state, 8, near_a)
    state = attend("far_a", state, 8, [far_a])
    side_b, beyond, state = lax.optimization_barrier((side_b, beyond, state))

    far_b = send(jnp.stack([with_either(c == 0), *side_b]), swap_core(size))
    state = attend("near_b", state, 8, [p34, *side_b])
    width = out_weight.shape[1] // 4
    share = jax.ShapeDtypeStruct((tokens, width), jnp.bfloat16)
    total, *shares = pl.pallas_call(
        last_kernel,
        out_shape=(jax.ShapeDtypeStruct(share.shape, jnp.float32), share, share, share),
        in_specs=[SMEM] + [VMEM] * 7,
        out_specs=(VMEM,) * 4,
        scratch_shapes=[pltpu.VMEM(queries.shape, queries.dtype)],
        compiler_params=params(16),
        cost_estimate=cost(9, rows, 2 * tokens * out_weight.shape[0] * out_weight.shape[1]),
        name="last",
    )(lane[None], heads, own, *state, far_b, beyond, out_weight)

    for k, part in zip((2, 1, 3), shares):
        got = lax.ppermute(part, "tp", [(i, i ^ k) for i in range(4)])
        total = total + got.astype(jnp.float32)
    return total.astype(jnp.bfloat16)


def solution(mesh):
    placed = (P("ctx", "tp"), P("ctx", "tp"), P("ctx", "tp"), P("ctx"), P("tp", None))
    return jax.shard_map(
        functools.partial(on_device, mesh.shape["ctx"]),
        mesh=mesh,
        in_specs=placed,
        out_specs=P("ctx", "tp"),
        check_vma=False,
    )
```

```python
import functools

import jax
import jax.numpy as jnp
from jax import lax
from jax.experimental import pallas as pl
from jax.experimental.pallas import tpu as pltpu
from jax.sharding import PartitionSpec as P

HEAD_DIM = 128
LOG2E = 1.4426950408889634
SCALE = HEAD_DIM ** (-0.5) * LOG2E
NEG = -1e30
ACC_ROWS = 144

VMEM = pl.BlockSpec(memory_space=pltpu.VMEM)
SMEM = pl.BlockSpec(memory_space=pltpu.SMEM)
HBM = pl.BlockSpec(memory_space=pltpu.HBM)


def ctx_pairs(size, target):
    pairs = [(i, target(i)) for i in range(size)]
    return [(i, k) for i, k in pairs if 0 <= k < size]


def shift_z(size, planes):
    return ctx_pairs(size, lambda i: i + 8 * planes)


def shift_x(size, steps):
    return ctx_pairs(size, lambda i: i // 8 * 8 + (i + 2 * steps) % 8)


def swap_core(size):
    return ctx_pairs(size, lambda i: i ^ 1)


def params(mebibytes):
    return pltpu.CompilerParams(vmem_limit_bytes=mebibytes * 1024 * 1024)


def cost(blocks, rows, more=0):
    return pl.CostEstimate(
        flops=blocks * 128 * rows * 128 * 128 + more,
        bytes_accessed=blocks * 65536,
        transcendentals=blocks * 128 * rows,
    )


def seg_row(block):
    return block[256:272].astype(jnp.float32)[0:1]


def column(row):
    return jnp.transpose(jnp.broadcast_to(row, (128, 128)))


def absorb(q, m, acc, blocks, allowed):
    keys = jnp.concatenate([b[0:128] for b in blocks], 0)
    values = jnp.concatenate([b[128:256] for b in blocks], 1)
    s = lax.dot_general(keys, q, (((1,), (1,)), ((), ())), preferred_element_type=jnp.float32)
    allowed = jnp.concatenate(allowed, 0)
    s = jnp.concatenate(
        [jnp.where(allowed, s[:, h : h + 128], NEG) for h in range(0, s.shape[1], 128)], 1
    )
    top = jnp.max(s, axis=0, keepdims=True)
    new_m = top if m is None else jnp.maximum(m, top)
    weight = jnp.exp2((s - new_m) * SCALE).astype(jnp.bfloat16)
    ones = jnp.ones((ACC_ROWS - 128, values.shape[1]), values.dtype)
    part = jnp.dot(
        jnp.concatenate([values, ones], 0), weight, preferred_element_type=jnp.float32
    )
    if m is not None:
        part = acc * jnp.exp2((m - new_m) * SCALE) + part
    return new_m, part


def pack_kernel(k_ref, v_ref, seg_ref, out_ref, v_buf, seg_buf, sems):
    copies = [
        pltpu.make_async_copy(k_ref, out_ref.at[0, 0:128, :], sems.at[0]),
        pltpu.make_async_copy(v_ref, v_buf, sems.at[1]),
        pltpu.make_async_copy(seg_ref, seg_buf, sems.at[2]),
    ]
    for copy in copies:
        copy.start()
    for copy in copies:
        copy.wait()
    out_ref[0, 128:256, :] = jnp.transpose(v_buf[...].astype(jnp.float32)).astype(out_ref.dtype)
    seg = (seg_buf[...] + 1).astype(jnp.float32)
    out_ref[0, 256:272, :] = jnp.broadcast_to(seg, (16, 128)).astype(out_ref.dtype)


def own_kernel(q_ref, own_ref, m_ref, acc_ref, heads_ref):
    width = q_ref.shape[1]
    q = jnp.concatenate(
        [q_ref[:, h * HEAD_DIM : (h + 1) * HEAD_DIM] for h in range(width // HEAD_DIM)], 0
    )
    heads_ref[...] = q
    own = own_ref[0]
    seg = seg_row(own)
    later = lax.broadcasted_iota(jnp.int32, (128, 128), 0) > lax.broadcasted_iota(
        jnp.int32, (128, 128), 1
    )
    allowed = (column(seg) == seg) & ~later
    m, acc = absorb(q, None, None, [own], [allowed])
    m_ref[...] = jnp.broadcast_to(m, m_ref.shape)
    acc_ref[...] = acc


def gather_blocks(refs):
    return [ref[(*lead,)] for ref in refs for lead in _leads(ref.shape[:-2])]


def _leads(shape):
    if not shape:
        return [()]
    return [(i, *rest) for i in range(shape[0]) for rest in _leads(shape[1:])]


def run(q_ref, own_ref, m_in, acc_in, refs):
    blocks = gather_blocks(refs)
    seg = seg_row(own_ref[0])
    allowed = [column(seg_row(block)) == seg for block in blocks]
    return absorb(q_ref[...], m_in[0:1], acc_in[...], blocks, allowed)


def group_kernel(q_ref, own_ref, m_in, acc_in, *rest):
    *refs, m_ref, acc_ref = rest
    m, acc = run(q_ref, own_ref, m_in, acc_in, refs)
    m_ref[...] = jnp.broadcast_to(m, m_ref.shape)
    acc_ref[...] = acc


def last_kernel(q_ref, own_ref, m_in, acc_in, far_ref, beyond_ref, att_ref):
    _, acc = run(q_ref, own_ref, m_in, acc_in, [far_ref, beyond_ref])
    result = acc[0:128] / acc[128:129]
    for h in range(q_ref.shape[0] // att_ref.shape[0]):
        part = slice(h * HEAD_DIM, (h + 1) * HEAD_DIM)
        att_ref[:, part] = jnp.transpose(result[:, part]).astype(att_ref.dtype)


def project_kernel(steps, lane_ref, att_ref, w_ref, *outs):
    for k, ref in zip(steps, outs):
        width = ref.shape[1]
        columns = pl.ds(pl.multiple_of((lane_ref[0] ^ k) * width, width), width)
        ref[...] = jnp.dot(
            att_ref[...], w_ref[:, columns], preferred_element_type=jnp.float32
        ).astype(ref.dtype)


def on_device(size, queries, keys, values, segment_ids, out_weight):
    tokens = queries.shape[0]
    rows = tokens * (queries.shape[1] // HEAD_DIM)
    index = lax.axis_index("ctx")
    lane = lax.axis_index("tp")
    x, c = index % 8 // 2, index % 2

    def send(value, pairs):
        return lax.ppermute(value, "ctx", pairs)

    own = pl.pallas_call(
        pack_kernel,
        out_shape=jax.ShapeDtypeStruct((1, 272, 128), jnp.bfloat16),
        in_specs=[HBM] * 3,
        out_specs=VMEM,
        scratch_shapes=[
            pltpu.VMEM((128, 128), jnp.bfloat16),
            pltpu.VMEM((1, 128), jnp.int32),
            pltpu.SemaphoreType.DMA((3,)),
        ],
        compiler_params=params(60),
        name="pack",
    )(keys, values, segment_ids[None])

    state_shape = (
        jax.ShapeDtypeStruct((8, rows), jnp.float32),
        jax.ShapeDtypeStruct((ACC_ROWS, rows), jnp.float32),
    )

    def attend(name, state, blocks, operands):
        return pl.pallas_call(
            group_kernel,
            out_shape=state_shape,
            in_specs=[VMEM] * (4 + len(operands)),
            out_specs=(VMEM, VMEM),
            compiler_params=params(16),
            cost_estimate=cost(blocks, rows),
            name=name,
        )(heads, own, *state, *operands)

    p2 = send(own, shift_z(size, 2))
    p1 = send(own, shift_z(size, 1))
    *state, heads = pl.pallas_call(
        own_kernel,
        out_shape=(*state_shape, jax.ShapeDtypeStruct((rows, HEAD_DIM), queries.dtype)),
        in_specs=[VMEM] * 2,
        out_specs=(VMEM,) * 3,
        compiler_params=params(12),
        cost_estimate=cost(1, rows),
        name="own",
    )(queries, own)
    p2, p1, state, heads = lax.optimization_barrier((p2, p1, state, heads))
    p12 = jnp.concatenate([p1, p2], 0)

    near_a = [p12] + [send(p12, shift_x(size, k)) for k in (2, 1, 3)]
    p34 = send(p12, shift_z(size, 2))
    p34, near_a[2], near_a[3], near_a[1], near_a[0] = lax.optimization_barrier(
        (p34, near_a[2], near_a[3], near_a[1], near_a[0])
    )

    def with_either(first):
        return jnp.concatenate([p34[0:1], jnp.where(first, own, p34[1:2])], 0)

    far_a = send(jnp.stack(near_a), swap_core(size))
    side_b = [send(with_either(x + k < 4), shift_x(size, k)) for k in (2, 1, 3)]
    beyond = send(p34[1:2], ctx_pairs(size, lambda i: i + 1))
    state = attend("near_a", state, 8, near_a)
    state = attend("far_a", state, 8, [far_a])
    side_b[1], side_b[2], side_b[0], beyond, state = lax.optimization_barrier(
        (side_b[1], side_b[2], side_b[0], beyond, state)
    )

    far_b = send(jnp.stack([with_either(c == 0), *side_b]), swap_core(size))
    state = attend("near_b", state, 8, [p34, *side_b])
    attention = pl.pallas_call(
        last_kernel,
        out_shape=jax.ShapeDtypeStruct(queries.shape, queries.dtype),
        in_specs=[VMEM] * 6,
        out_specs=VMEM,
        compiler_params=params(16),
        cost_estimate=cost(9, rows),
        name="last",
    )(heads, own, *state, far_b, beyond)

    width = out_weight.shape[1] // 4

    def project(name, steps, dtypes):
        return pl.pallas_call(
            functools.partial(project_kernel, steps),
            out_shape=tuple(jax.ShapeDtypeStruct((tokens, width), dtype) for dtype in dtypes),
            in_specs=[SMEM] + [VMEM] * 2,
            out_specs=(VMEM,) * len(steps),
            compiler_params=params(8),
            cost_estimate=pl.CostEstimate(
                flops=2 * len(steps) * tokens * width * out_weight.shape[0],
                bytes_accessed=2 * len(steps) * width * out_weight.shape[0],
                transcendentals=0,
            ),
            name=name,
        )(lane[None], attention, out_weight)

    def pass_on(part, k):
        return lax.ppermute(part, "tp", [(i, i ^ k) for i in range(4)])

    share_2, share_1, share_3, total = project(
        "project", (2, 1, 3, 0), (*[jnp.bfloat16] * 3, jnp.float32)
    )
    for k, part in ((2, share_2), (1, share_1), (3, share_3)):
        total = total + pass_on(part, k).astype(jnp.float32)
    return total.astype(jnp.bfloat16)


def solution(mesh):
    placed = (P("ctx", "tp"), P("ctx", "tp"), P("ctx", "tp"), P("ctx"), P("tp", None))
    return jax.shard_map(
        functools.partial(on_device, mesh.shape["ctx"]),
        mesh=mesh,
        in_specs=placed,
        out_specs=P("ctx", "tp"),
        check_vma=False,
    )
```

```python
import functools

import jax
import jax.numpy as jnp
from jax import lax
from jax.experimental import pallas as pl
from jax.experimental.pallas import tpu as pltpu
from jax.sharding import PartitionSpec as P

HEAD_DIM = 128
LOG2E = 1.4426950408889634
SCALE = HEAD_DIM ** (-0.5) * LOG2E
NEG = -1e30
ACC_ROWS = 144

VMEM = pl.BlockSpec(memory_space=pltpu.VMEM)
SMEM = pl.BlockSpec(memory_space=pltpu.SMEM)
HBM = pl.BlockSpec(memory_space=pltpu.HBM)


def ctx_pairs(size, target):
    pairs = [(i, target(i)) for i in range(size)]
    return [(i, k) for i, k in pairs if 0 <= k < size]


def shift_z(size, planes):
    return ctx_pairs(size, lambda i: (i + 8 * planes) % size)


def shift_x(size, steps):
    return ctx_pairs(size, lambda i: i // 8 * 8 + (i + 2 * steps) % 8)


def swap_core(size):
    return ctx_pairs(size, lambda i: i ^ 1)


def params(mebibytes):
    return pltpu.CompilerParams(vmem_limit_bytes=mebibytes * 1024 * 1024)


def cost(blocks, rows, more=0):
    return pl.CostEstimate(
        flops=blocks * 128 * rows * 128 * 128 + more,
        bytes_accessed=blocks * 65536,
        transcendentals=blocks * 128 * rows,
    )


def seg_row(block):
    return block[256:272].astype(jnp.float32)[0:1]


def column(row):
    return jnp.transpose(jnp.broadcast_to(row, (128, 128)))


def absorb(q, m, acc, blocks, allowed):
    keys = jnp.concatenate([b[0:128] for b in blocks], 0)
    values = jnp.concatenate([b[128:256] for b in blocks], 1)
    s = lax.dot_general(keys, q, (((1,), (1,)), ((), ())), preferred_element_type=jnp.float32)
    allowed = jnp.concatenate(allowed, 0)
    s = jnp.concatenate(
        [jnp.where(allowed, s[:, h : h + 128], NEG) for h in range(0, s.shape[1], 128)], 1
    )
    top = jnp.max(s, axis=0, keepdims=True)
    new_m = top if m is None else jnp.maximum(m, top)
    weight = jnp.exp2((s - new_m) * SCALE).astype(jnp.bfloat16)
    ones = jnp.ones((ACC_ROWS - 128, values.shape[1]), values.dtype)
    part = jnp.dot(
        jnp.concatenate([values, ones], 0), weight, preferred_element_type=jnp.float32
    )
    if m is not None:
        part = acc * jnp.exp2((m - new_m) * SCALE) + part
    return new_m, part


def pack_kernel(k_ref, v_ref, seg_ref, out_ref, v_buf, seg_buf, sems):
    copies = [
        pltpu.make_async_copy(k_ref, out_ref.at[0, 0:128, :], sems.at[0]),
        pltpu.make_async_copy(v_ref, v_buf, sems.at[1]),
        pltpu.make_async_copy(seg_ref, seg_buf, sems.at[2]),
    ]
    for copy in copies:
        copy.start()
    for copy in copies:
        copy.wait()
    out_ref[0, 128:256, :] = jnp.transpose(v_buf[...].astype(jnp.float32)).astype(out_ref.dtype)
    seg = (seg_buf[...] + 1).astype(jnp.float32)
    out_ref[0, 256:272, :] = jnp.broadcast_to(seg, (16, 128)).astype(out_ref.dtype)


def own_kernel(q_ref, own_ref, m_ref, acc_ref, heads_ref):
    width = q_ref.shape[1]
    q = jnp.concatenate(
        [q_ref[:, h * HEAD_DIM : (h + 1) * HEAD_DIM] for h in range(width // HEAD_DIM)], 0
    )
    heads_ref[...] = q
    own = own_ref[0]
    seg = seg_row(own)
    later = lax.broadcasted_iota(jnp.int32, (128, 128), 0) > lax.broadcasted_iota(
        jnp.int32, (128, 128), 1
    )
    allowed = (column(seg) == seg) & ~later
    m, acc = absorb(q, None, None, [own], [allowed])
    m_ref[...] = jnp.broadcast_to(m, m_ref.shape)
    acc_ref[...] = acc


def gather_blocks(refs):
    return [ref[(*lead,)] for ref in refs for lead in _leads(ref.shape[:-2])]


def _leads(shape):
    if not shape:
        return [()]
    return [(i, *rest) for i in range(shape[0]) for rest in _leads(shape[1:])]


def run(q_ref, own_ref, m_in, acc_in, refs):
    blocks = gather_blocks(refs)
    seg = seg_row(own_ref[0])
    allowed = [column(seg_row(block)) == seg for block in blocks]
    return absorb(q_ref[...], m_in[0:1], acc_in[...], blocks, allowed)


def group_kernel(q_ref, own_ref, m_in, acc_in, *rest):
    *refs, m_ref, acc_ref = rest
    m, acc = run(q_ref, own_ref, m_in, acc_in, refs)
    m_ref[...] = jnp.broadcast_to(m, m_ref.shape)
    acc_ref[...] = acc


def last_kernel(q_ref, own_ref, m_in, acc_in, far_ref, beyond_ref, att_ref):
    _, acc = run(q_ref, own_ref, m_in, acc_in, [far_ref, beyond_ref])
    result = acc[0:128] / acc[128:129]
    for h in range(q_ref.shape[0] // att_ref.shape[0]):
        part = slice(h * HEAD_DIM, (h + 1) * HEAD_DIM)
        att_ref[:, part] = jnp.transpose(result[:, part]).astype(att_ref.dtype)


def project_kernel(steps, lane_ref, att_ref, w_ref, *outs):
    for k, ref in zip(steps, outs):
        width = ref.shape[1]
        columns = pl.ds(pl.multiple_of((lane_ref[0] ^ k) * width, width), width)
        ref[...] = jnp.dot(
            att_ref[...], w_ref[:, columns], preferred_element_type=jnp.float32
        ).astype(ref.dtype)


def on_device(size, queries, keys, values, segment_ids, out_weight):
    tokens = queries.shape[0]
    rows = tokens * (queries.shape[1] // HEAD_DIM)
    index = lax.axis_index("ctx")
    lane = lax.axis_index("tp")
    z, x, c = index // 8, index % 8 // 2, index % 2

    def send(value, pairs):
        return lax.ppermute(value, "ctx", pairs)

    own = pl.pallas_call(
        pack_kernel,
        out_shape=jax.ShapeDtypeStruct((1, 272, 128), jnp.bfloat16),
        in_specs=[HBM] * 3,
        out_specs=VMEM,
        scratch_shapes=[
            pltpu.VMEM((128, 128), jnp.bfloat16),
            pltpu.VMEM((1, 128), jnp.int32),
            pltpu.SemaphoreType.DMA((3,)),
        ],
        compiler_params=params(60),
        name="pack",
    )(keys, values, segment_ids[None])

    state_shape = (
        jax.ShapeDtypeStruct((8, rows), jnp.float32),
        jax.ShapeDtypeStruct((ACC_ROWS, rows), jnp.float32),
    )

    def attend(name, state, blocks, operands):
        return pl.pallas_call(
            group_kernel,
            out_shape=state_shape,
            in_specs=[VMEM] * (4 + len(operands)),
            out_specs=(VMEM, VMEM),
            compiler_params=params(16),
            cost_estimate=cost(blocks, rows),
            name=name,
        )(heads, own, *state, *operands)

    p2 = send(own, shift_z(size, 2))
    p1 = send(own, shift_z(size, 1))
    *state, heads = pl.pallas_call(
        own_kernel,
        out_shape=(*state_shape, jax.ShapeDtypeStruct((rows, HEAD_DIM), queries.dtype)),
        in_specs=[VMEM] * 2,
        out_specs=(VMEM,) * 3,
        compiler_params=params(12),
        cost_estimate=cost(1, rows),
        name="own",
    )(queries, own)
    p2, p1, state, heads = lax.optimization_barrier((p2, p1, state, heads))
    p12 = jnp.concatenate([p1, p2], 0)

    near_a = [p12] + [send(p12, shift_x(size, k)) for k in (2, 1, 3)]
    onward = z < size // 8 - 2
    p12_on = jnp.concatenate(
        [jnp.where(onward & (z >= 1), p1, 0), jnp.where(onward & (z >= 2), p2, 0)], 0
    )
    p34 = send(p12_on, shift_z(size, 2))
    p34, near_a[2], near_a[3], near_a[1], near_a[0] = lax.optimization_barrier(
        (p34, near_a[2], near_a[3], near_a[1], near_a[0])
    )

    def with_either(first):
        return jnp.concatenate([p34[0:1], jnp.where(first, own, p34[1:2])], 0)

    side_b = [send(with_either(x + k < 4), shift_x(size, k)) for k in (2, 1, 3)]
    beyond = send(p34[1:2], [(i, i + 1) for i in range(32, size - 1)])
    far_a = send(jnp.stack(near_a), swap_core(size))
    state = attend("near_a", state, 8, near_a)
    state = attend("far_a", state, 8, [far_a])
    side_b[1], side_b[2], side_b[0], beyond, state = lax.optimization_barrier(
        (side_b[1], side_b[2], side_b[0], beyond, state)
    )

    far_b = send(jnp.stack([with_either(c == 0), *side_b]), swap_core(size))
    state = attend("near_b", state, 8, [p34, *side_b])
    attention = pl.pallas_call(
        last_kernel,
        out_shape=jax.ShapeDtypeStruct(queries.shape, queries.dtype),
        in_specs=[VMEM] * 6,
        out_specs=VMEM,
        compiler_params=params(16),
        cost_estimate=cost(9, rows),
        name="last",
    )(heads, own, *state, far_b, beyond)

    width = out_weight.shape[1] // 4

    def project(name, steps, dtypes):
        return pl.pallas_call(
            functools.partial(project_kernel, steps),
            out_shape=tuple(jax.ShapeDtypeStruct((tokens, width), dtype) for dtype in dtypes),
            in_specs=[SMEM] + [VMEM] * 2,
            out_specs=(VMEM,) * len(steps),
            compiler_params=params(8),
            cost_estimate=pl.CostEstimate(
                flops=2 * len(steps) * tokens * width * out_weight.shape[0],
                bytes_accessed=2 * len(steps) * width * out_weight.shape[0],
                transcendentals=0,
            ),
            name=name,
        )(lane[None], attention, out_weight)

    def pass_on(part, k):
        return lax.ppermute(part, "tp", [(i, i ^ k) for i in range(4)])

    share_2, share_1, share_3, total = project(
        "project", (2, 1, 3, 0), (*[jnp.bfloat16] * 3, jnp.float32)
    )
    for k, part in ((2, share_2), (1, share_1), (3, share_3)):
        total = total + pass_on(part, k).astype(jnp.float32)
    return total.astype(jnp.bfloat16)


def solution(mesh):
    placed = (P("ctx", "tp"), P("ctx", "tp"), P("ctx", "tp"), P("ctx"), P("tp", None))
    return jax.shard_map(
        functools.partial(on_device, mesh.shape["ctx"]),
        mesh=mesh,
        in_specs=placed,
        out_specs=P("ctx", "tp"),
        check_vma=False,
    )
```

```python
import functools

import jax
import jax.numpy as jnp
from jax import lax
from jax.experimental import pallas as pl
from jax.experimental.pallas import tpu as pltpu
from jax.sharding import PartitionSpec as P

HEAD_DIM = 128
LOG2E = 1.4426950408889634
SCALE = HEAD_DIM ** (-0.5) * LOG2E
NEG = -1e30
ACC_ROWS = 144

VMEM = pl.BlockSpec(memory_space=pltpu.VMEM)
SMEM = pl.BlockSpec(memory_space=pltpu.SMEM)
HBM = pl.BlockSpec(memory_space=pltpu.HBM)


def ctx_pairs(size, target):
    pairs = [(i, target(i)) for i in range(size)]
    return [(i, k) for i, k in pairs if 0 <= k < size]


def shift_z(size, planes):
    return ctx_pairs(size, lambda i: (i + 8 * planes) % size)


def shift_x(size, steps):
    return ctx_pairs(size, lambda i: i // 8 * 8 + (i + 2 * steps) % 8)


def swap_core(size):
    return ctx_pairs(size, lambda i: i ^ 1)


def params(mebibytes):
    return pltpu.CompilerParams(vmem_limit_bytes=mebibytes * 1024 * 1024)


def cost(blocks, rows, more=0):
    return pl.CostEstimate(
        flops=blocks * 128 * rows * 128 * 128 + more,
        bytes_accessed=blocks * 65536,
        transcendentals=blocks * 128 * rows,
    )


def seg_row(block):
    return block[256:272].astype(jnp.float32)[0:1]


def column(row):
    return jnp.transpose(jnp.broadcast_to(row, (128, 128)))


def absorb(q, m, acc, blocks, allowed):
    keys = jnp.concatenate([b[0:128] for b in blocks], 0)
    values = jnp.concatenate([b[128:256] for b in blocks], 1)
    s = lax.dot_general(keys, q, (((1,), (1,)), ((), ())), preferred_element_type=jnp.float32)
    allowed = jnp.concatenate(allowed, 0)
    s = jnp.concatenate(
        [jnp.where(allowed, s[:, h : h + 128], NEG) for h in range(0, s.shape[1], 128)], 1
    )
    top = jnp.max(s, axis=0, keepdims=True)
    new_m = top if m is None else jnp.maximum(m, top)
    weight = jnp.exp2((s - new_m) * SCALE).astype(jnp.bfloat16)
    ones = jnp.ones((ACC_ROWS - 128, values.shape[1]), values.dtype)
    part = jnp.dot(
        jnp.concatenate([values, ones], 0), weight, preferred_element_type=jnp.float32
    )
    if m is not None:
        part = acc * jnp.exp2((m - new_m) * SCALE) + part
    return new_m, part


def pack_kernel(k_ref, v_ref, seg_ref, out_ref, v_buf, seg_buf, sems):
    copies = [
        pltpu.make_async_copy(k_ref, out_ref.at[0, 0:128, :], sems.at[0]),
        pltpu.make_async_copy(v_ref, v_buf, sems.at[1]),
        pltpu.make_async_copy(seg_ref, seg_buf, sems.at[2]),
    ]
    for copy in copies:
        copy.start()
    for copy in copies:
        copy.wait()
    out_ref[0, 128:256, :] = jnp.transpose(v_buf[...].astype(jnp.float32)).astype(out_ref.dtype)
    seg = (seg_buf[...] + 1).astype(jnp.float32)
    out_ref[0, 256:272, :] = jnp.broadcast_to(seg, (16, 128)).astype(out_ref.dtype)


def own_kernel(q_ref, own_ref, m_ref, acc_ref, heads_ref):
    width = q_ref.shape[1]
    q = jnp.concatenate(
        [q_ref[:, h * HEAD_DIM : (h + 1) * HEAD_DIM] for h in range(width // HEAD_DIM)], 0
    )
    heads_ref[...] = q
    own = own_ref[0]
    seg = seg_row(own)
    later = lax.broadcasted_iota(jnp.int32, (128, 128), 0) > lax.broadcasted_iota(
        jnp.int32, (128, 128), 1
    )
    allowed = (column(seg) == seg) & ~later
    m, acc = absorb(q, None, None, [own], [allowed])
    m_ref[...] = jnp.broadcast_to(m, m_ref.shape)
    acc_ref[...] = acc


def gather_blocks(refs):
    return [ref[(*lead,)] for ref in refs for lead in _leads(ref.shape[:-2])]


def _leads(shape):
    if not shape:
        return [()]
    return [(i, *rest) for i in range(shape[0]) for rest in _leads(shape[1:])]


def run(q_ref, own_ref, m_in, acc_in, refs):
    blocks = gather_blocks(refs)
    seg = seg_row(own_ref[0])
    allowed = [column(seg_row(block)) == seg for block in blocks]
    return absorb(q_ref[...], m_in[0:1], acc_in[...], blocks, allowed)


def group_kernel(q_ref, own_ref, m_in, acc_in, *rest):
    *refs, m_ref, acc_ref = rest
    m, acc = run(q_ref, own_ref, m_in, acc_in, refs)
    m_ref[...] = jnp.broadcast_to(m, m_ref.shape)
    acc_ref[...] = acc


def last_kernel(q_ref, own_ref, m_in, acc_in, far_ref, beyond_ref, att_ref):
    _, acc = run(q_ref, own_ref, m_in, acc_in, [far_ref, beyond_ref])
    result = acc[0:128] / acc[128:129]
    for h in range(q_ref.shape[0] // att_ref.shape[0]):
        part = slice(h * HEAD_DIM, (h + 1) * HEAD_DIM)
        att_ref[:, part] = jnp.transpose(result[:, part]).astype(att_ref.dtype)


def project_kernel(steps, lane_ref, att_ref, w_ref, *outs):
    for k, ref in zip(steps, outs):
        width = ref.shape[1]
        columns = pl.ds(pl.multiple_of((lane_ref[0] ^ k) * width, width), width)
        ref[...] = jnp.dot(
            att_ref[...], w_ref[:, columns], preferred_element_type=jnp.float32
        ).astype(ref.dtype)


def on_device(size, queries, keys, values, segment_ids, out_weight):
    tokens = queries.shape[0]
    rows = tokens * (queries.shape[1] // HEAD_DIM)
    index = lax.axis_index("ctx")
    lane = lax.axis_index("tp")
    z, x, c = index // 8, index % 8 // 2, index % 2

    def send(value, pairs):
        return lax.ppermute(value, "ctx", pairs)

    own = pl.pallas_call(
        pack_kernel,
        out_shape=jax.ShapeDtypeStruct((1, 272, 128), jnp.bfloat16),
        in_specs=[HBM] * 3,
        out_specs=VMEM,
        scratch_shapes=[
            pltpu.VMEM((128, 128), jnp.bfloat16),
            pltpu.VMEM((1, 128), jnp.int32),
            pltpu.SemaphoreType.DMA((3,)),
        ],
        compiler_params=params(60),
        name="pack",
    )(keys, values, segment_ids[None])

    state_shape = (
        jax.ShapeDtypeStruct((8, rows), jnp.float32),
        jax.ShapeDtypeStruct((ACC_ROWS, rows), jnp.float32),
    )

    def attend(name, state, blocks, operands):
        return pl.pallas_call(
            group_kernel,
            out_shape=state_shape,
            in_specs=[VMEM] * (4 + len(operands)),
            out_specs=(VMEM, VMEM),
            compiler_params=params(16),
            cost_estimate=cost(blocks, rows),
            name=name,
        )(heads, own, *state, *operands)

    p1 = send(own, shift_z(size, 1))
    p2 = send(own, shift_z(size, 2))
    *state, heads = pl.pallas_call(
        own_kernel,
        out_shape=(*state_shape, jax.ShapeDtypeStruct((rows, HEAD_DIM), queries.dtype)),
        in_specs=[VMEM] * 2,
        out_specs=(VMEM,) * 3,
        compiler_params=params(12),
        cost_estimate=cost(1, rows),
        name="own",
    )(queries, own)
    p1, p2, state, heads = lax.optimization_barrier((p1, p2, state, heads))
    p12 = jnp.concatenate([p1, p2], 0)

    near_a = [p12] + [send(p12, shift_x(size, k)) for k in (2, 1, 3)]
    onward = z < size // 8 - 2
    p12_on = jnp.concatenate(
        [jnp.where(onward & (z >= 1), p1, 0), jnp.where(onward & (z >= 2), p2, 0)], 0
    )
    p34 = send(p12_on, shift_z(size, 2))
    p34, near_a[2], near_a[3], near_a[1], near_a[0] = lax.optimization_barrier(
        (p34, near_a[2], near_a[3], near_a[1], near_a[0])
    )

    def with_either(first):
        return jnp.concatenate([p34[0:1], jnp.where(first, own, p34[1:2])], 0)

    side_b = [send(with_either(x + k < 4), shift_x(size, k)) for k in (2, 1, 3)]
    beyond = send(p34[1:2], [(i, i + 1) for i in range(32, size - 1)])
    far_a = send(jnp.stack(near_a), swap_core(size))
    state = attend("near_a", state, 8, near_a)
    state = attend("far_a", state, 10, [far_a, p34])
    side_b[1], side_b[2], side_b[0], beyond, state = lax.optimization_barrier(
        (side_b[1], side_b[2], side_b[0], beyond, state)
    )

    far_b = send(jnp.stack([with_either(c == 0), *side_b]), swap_core(size))
    state = attend("near_b", state, 6, side_b)
    attention = pl.pallas_call(
        last_kernel,
        out_shape=jax.ShapeDtypeStruct(queries.shape, queries.dtype),
        in_specs=[VMEM] * 6,
        out_specs=VMEM,
        compiler_params=params(16),
        cost_estimate=cost(9, rows),
        name="last",
    )(heads, own, *state, far_b, beyond)

    width = out_weight.shape[1] // 4

    def project(name, steps, dtypes, weigh=1):
        return pl.pallas_call(
            functools.partial(project_kernel, steps),
            out_shape=tuple(jax.ShapeDtypeStruct((tokens, width), dtype) for dtype in dtypes),
            in_specs=[SMEM] + [VMEM] * 2,
            out_specs=(VMEM,) * len(steps),
            compiler_params=params(8),
            cost_estimate=pl.CostEstimate(
                flops=weigh * 2 * len(steps) * tokens * width * out_weight.shape[0],
                bytes_accessed=2 * len(steps) * width * out_weight.shape[0],
                transcendentals=0,
            ),
            name=name,
        )(lane[None], attention, out_weight)

    def pass_on(part, k):
        return lax.ppermute(part, "tp", [(i, i ^ k) for i in range(4)])

    (share_2,) = project("project_2", (2,), [jnp.bfloat16])
    got_2 = pass_on(share_2, 2)
    _, attention = lax.optimization_barrier((share_2, attention))
    share_1, share_3 = project("project_1_3", (1, 3), [jnp.bfloat16] * 2, 64)
    (total,) = project("project_own", (0,), (jnp.float32,), 64)
    for got in (got_2, pass_on(share_1, 1), pass_on(share_3, 3)):
        total = total + got.astype(jnp.float32)
    return total.astype(jnp.bfloat16)


def solution(mesh):
    placed = (P("ctx", "tp"), P("ctx", "tp"), P("ctx", "tp"), P("ctx"), P("tp", None))
    return jax.shard_map(
        functools.partial(on_device, mesh.shape["ctx"]),
        mesh=mesh,
        in_specs=placed,
        out_specs=P("ctx", "tp"),
        check_vma=False,
    )
```

```python
import functools

import jax
import jax.numpy as jnp
from jax import lax
from jax.experimental import pallas as pl
from jax.experimental.pallas import tpu as pltpu
from jax.sharding import PartitionSpec as P

HEAD_DIM = 128
LOG2E = 1.4426950408889634
SCALE = HEAD_DIM ** (-0.5) * LOG2E
NEG = -1e30
ACC_ROWS = 144

VMEM = pl.BlockSpec(memory_space=pltpu.VMEM)
SMEM = pl.BlockSpec(memory_space=pltpu.SMEM)
HBM = pl.BlockSpec(memory_space=pltpu.HBM)


def ctx_pairs(size, target):
    pairs = [(i, target(i)) for i in range(size)]
    return [(i, k) for i, k in pairs if 0 <= k < size]


def shift_z(size, planes):
    return ctx_pairs(size, lambda i: (i + 8 * planes) % size)


def shift_x(size, steps):
    return ctx_pairs(size, lambda i: i // 8 * 8 + (i + 2 * steps) % 8)


def swap_core(size):
    return ctx_pairs(size, lambda i: i ^ 1)


def params(mebibytes):
    return pltpu.CompilerParams(vmem_limit_bytes=mebibytes * 1024 * 1024)


def cost(blocks, rows, more=0):
    return pl.CostEstimate(
        flops=blocks * 128 * rows * 128 * 128 + more,
        bytes_accessed=blocks * 65536,
        transcendentals=blocks * 128 * rows,
    )


def seg_row(block):
    return block[256:272].astype(jnp.float32)[0:1]


def column(row):
    return jnp.transpose(jnp.broadcast_to(row, (128, 128)))


def absorb(q, m, acc, blocks, allowed):
    keys = jnp.concatenate([b[0:128] for b in blocks], 0)
    values = jnp.concatenate([b[128:256] for b in blocks], 1)
    s = lax.dot_general(keys, q, (((1,), (1,)), ((), ())), preferred_element_type=jnp.float32)
    allowed = jnp.concatenate(allowed, 0)
    s = jnp.concatenate(
        [jnp.where(allowed, s[:, h : h + 128], NEG) for h in range(0, s.shape[1], 128)], 1
    )
    top = jnp.max(s, axis=0, keepdims=True)
    new_m = top if m is None else jnp.maximum(m, top)
    weight = jnp.exp2((s - new_m) * SCALE).astype(jnp.bfloat16)
    ones = jnp.ones((ACC_ROWS - 128, values.shape[1]), values.dtype)
    part = jnp.dot(
        jnp.concatenate([values, ones], 0), weight, preferred_element_type=jnp.float32
    )
    if m is not None:
        part = acc * jnp.exp2((m - new_m) * SCALE) + part
    return new_m, part


def pack_kernel(k_ref, v_ref, seg_ref, out_ref, v_buf, seg_buf, sems):
    copies = [
        pltpu.make_async_copy(k_ref, out_ref.at[0, 0:128, :], sems.at[0]),
        pltpu.make_async_copy(v_ref, v_buf, sems.at[1]),
        pltpu.make_async_copy(seg_ref, seg_buf, sems.at[2]),
    ]
    for copy in copies:
        copy.start()
    for copy in copies:
        copy.wait()
    out_ref[0, 128:256, :] = jnp.transpose(v_buf[...].astype(jnp.float32)).astype(out_ref.dtype)
    seg = (seg_buf[...] + 1).astype(jnp.float32)
    out_ref[0, 256:272, :] = jnp.broadcast_to(seg, (16, 128)).astype(out_ref.dtype)


def own_kernel(q_ref, own_ref, m_ref, acc_ref, heads_ref):
    width = q_ref.shape[1]
    q = jnp.concatenate(
        [q_ref[:, h * HEAD_DIM : (h + 1) * HEAD_DIM] for h in range(width // HEAD_DIM)], 0
    )
    heads_ref[...] = q
    own = own_ref[0]
    seg = seg_row(own)
    later = lax.broadcasted_iota(jnp.int32, (128, 128), 0) > lax.broadcasted_iota(
        jnp.int32, (128, 128), 1
    )
    allowed = (column(seg) == seg) & ~later
    m, acc = absorb(q, None, None, [own], [allowed])
    m_ref[...] = jnp.broadcast_to(m, m_ref.shape)
    acc_ref[...] = acc


def gather_blocks(refs):
    return [ref[(*lead,)] for ref in refs for lead in _leads(ref.shape[:-2])]


def _leads(shape):
    if not shape:
        return [()]
    return [(i, *rest) for i in range(shape[0]) for rest in _leads(shape[1:])]


def run(q_ref, own_ref, m_in, acc_in, refs):
    blocks = gather_blocks(refs)
    seg = seg_row(own_ref[0])
    allowed = [column(seg_row(block)) == seg for block in blocks]
    return absorb(q_ref[...], m_in[0:1], acc_in[...], blocks, allowed)


def group_kernel(q_ref, own_ref, m_in, acc_in, *rest):
    *refs, m_ref, acc_ref = rest
    m, acc = run(q_ref, own_ref, m_in, acc_in, refs)
    m_ref[...] = jnp.broadcast_to(m, m_ref.shape)
    acc_ref[...] = acc


def last_kernel(q_ref, own_ref, m_in, acc_in, far_ref, att_ref):
    _, acc = run(q_ref, own_ref, m_in, acc_in, [far_ref])
    result = acc[0:128] / acc[128:129]
    for h in range(q_ref.shape[0] // att_ref.shape[0]):
        part = slice(h * HEAD_DIM, (h + 1) * HEAD_DIM)
        att_ref[:, part] = jnp.transpose(result[:, part]).astype(att_ref.dtype)


def project_kernel(steps, lane_ref, att_ref, w_ref, *outs):
    for k, ref in zip(steps, outs):
        width = ref.shape[1]
        columns = pl.ds(pl.multiple_of((lane_ref[0] ^ k) * width, width), width)
        ref[...] = jnp.dot(
            att_ref[...], w_ref[:, columns], preferred_element_type=jnp.float32
        ).astype(ref.dtype)


def on_device(size, queries, keys, values, segment_ids, out_weight):
    tokens = queries.shape[0]
    rows = tokens * (queries.shape[1] // HEAD_DIM)
    index = lax.axis_index("ctx")
    lane = lax.axis_index("tp")
    z, x, c = index // 8, index % 8 // 2, index % 2

    def send(value, pairs):
        return lax.ppermute(value, "ctx", pairs)

    own = pl.pallas_call(
        pack_kernel,
        out_shape=jax.ShapeDtypeStruct((1, 272, 128), jnp.bfloat16),
        in_specs=[HBM] * 3,
        out_specs=VMEM,
        scratch_shapes=[
            pltpu.VMEM((128, 128), jnp.bfloat16),
            pltpu.VMEM((1, 128), jnp.int32),
            pltpu.SemaphoreType.DMA((3,)),
        ],
        compiler_params=params(60),
        name="pack",
    )(keys, values, segment_ids[None])

    state_shape = (
        jax.ShapeDtypeStruct((8, rows), jnp.float32),
        jax.ShapeDtypeStruct((ACC_ROWS, rows), jnp.float32),
    )

    def attend(name, state, blocks, operands):
        return pl.pallas_call(
            group_kernel,
            out_shape=state_shape,
            in_specs=[VMEM] * (4 + len(operands)),
            out_specs=(VMEM, VMEM),
            compiler_params=params(16),
            cost_estimate=cost(blocks, rows),
            name=name,
        )(heads, own, *state, *operands)

    p1 = send(own, shift_z(size, 1))
    p2 = send(own, shift_z(size, 2))
    *state, heads = pl.pallas_call(
        own_kernel,
        out_shape=(*state_shape, jax.ShapeDtypeStruct((rows, HEAD_DIM), queries.dtype)),
        in_specs=[VMEM] * 2,
        out_specs=(VMEM,) * 3,
        compiler_params=params(12),
        cost_estimate=cost(1, rows),
        name="own",
    )(queries, own)
    p1, p2, state, heads = lax.optimization_barrier((p1, p2, state, heads))
    p12 = jnp.concatenate([p1, p2], 0)

    near_a = [p12] + [send(p12, shift_x(size, k)) for k in (2, 1, 3)]
    onward = z < size // 8 - 2
    p12_on = jnp.concatenate(
        [jnp.where(onward & (z >= 1), p1, 0), jnp.where(onward & (z >= 2), p2, 0)], 0
    )
    p34 = send(p12_on, shift_z(size, 2))
    p34, near_a[2], near_a[3], near_a[1], near_a[0] = lax.optimization_barrier(
        (p34, near_a[2], near_a[3], near_a[1], near_a[0])
    )

    def with_either(first):
        return jnp.concatenate([p34[0:1], jnp.where(first, own, p34[1:2])], 0)

    side_b = [send(with_either(x + k < 4), shift_x(size, k)) for k in (2, 1, 3)]
    beyond = send(p34[1:2], [(i, i + 1) for i in range(32, size - 1)])
    far_a = send(jnp.stack(near_a), swap_core(size))
    state = attend("near_a", state, 8, near_a)
    state = attend("far_a", state, 10, [far_a, p34])
    side_b[1], side_b[2], side_b[0], beyond, state = lax.optimization_barrier(
        (side_b[1], side_b[2], side_b[0], beyond, state)
    )

    far_b = send(jnp.stack([with_either(c == 0), *side_b]), swap_core(size))
    state = attend("near_b", state, 7, [*side_b, beyond])
    attention = pl.pallas_call(
        last_kernel,
        out_shape=jax.ShapeDtypeStruct(queries.shape, queries.dtype),
        in_specs=[VMEM] * 5,
        out_specs=VMEM,
        compiler_params=params(16),
        cost_estimate=cost(8, rows),
        name="last",
    )(heads, own, *state, far_b)

    width = out_weight.shape[1] // 4

    def project(name, steps, dtypes, weigh=1):
        return pl.pallas_call(
            functools.partial(project_kernel, steps),
            out_shape=tuple(jax.ShapeDtypeStruct((tokens, width), dtype) for dtype in dtypes),
            in_specs=[SMEM] + [VMEM] * 2,
            out_specs=(VMEM,) * len(steps),
            compiler_params=params(8),
            cost_estimate=pl.CostEstimate(
                flops=weigh * 2 * len(steps) * tokens * width * out_weight.shape[0],
                bytes_accessed=2 * len(steps) * width * out_weight.shape[0],
                transcendentals=0,
            ),
            name=name,
        )(lane[None], attention, out_weight)

    def pass_on(part, k):
        return lax.ppermute(part, "tp", [(i, i ^ k) for i in range(4)])

    (share_2,) = project("project_2", (2,), [jnp.bfloat16])
    got_2 = pass_on(share_2, 2)
    _, attention = lax.optimization_barrier((share_2, attention))
    share_1, share_3 = project("project_1_3", (1, 3), [jnp.bfloat16] * 2, 64)
    (total,) = project("project_own", (0,), (jnp.float32,), 64)
    for got in (got_2, pass_on(share_1, 1), pass_on(share_3, 3)):
        total = total + got.astype(jnp.float32)
    return total.astype(jnp.bfloat16)


def solution(mesh):
    placed = (P("ctx", "tp"), P("ctx", "tp"), P("ctx", "tp"), P("ctx"), P("tp", None))
    return jax.shard_map(
        functools.partial(on_device, mesh.shape["ctx"]),
        mesh=mesh,
        in_specs=placed,
        out_specs=P("ctx", "tp"),
        check_vma=False,
    )
```

```python
import functools

import jax
import jax.numpy as jnp
from jax import lax
from jax.experimental import pallas as pl
from jax.experimental.pallas import tpu as pltpu
from jax.sharding import PartitionSpec as P

HEAD_DIM = 128
LOG2E = 1.4426950408889634
SCALE = HEAD_DIM ** (-0.5) * LOG2E
NEG = -1e30
ACC_ROWS = 144

VMEM = pl.BlockSpec(memory_space=pltpu.VMEM)
SMEM = pl.BlockSpec(memory_space=pltpu.SMEM)
HBM = pl.BlockSpec(memory_space=pltpu.HBM)


def ctx_pairs(size, target):
    pairs = [(i, target(i)) for i in range(size)]
    return [(i, k) for i, k in pairs if 0 <= k < size]


def shift_z(size, planes):
    return ctx_pairs(size, lambda i: (i + 8 * planes) % size)


def shift_x(size, steps):
    return ctx_pairs(size, lambda i: i // 8 * 8 + (i + 2 * steps) % 8)


def swap_core(size):
    return ctx_pairs(size, lambda i: i ^ 1)


def params(mebibytes):
    return pltpu.CompilerParams(vmem_limit_bytes=mebibytes * 1024 * 1024)


def cost(blocks, rows, more=0):
    return pl.CostEstimate(
        flops=blocks * 128 * rows * 128 * 128 + more,
        bytes_accessed=blocks * 65536,
        transcendentals=blocks * 128 * rows,
    )


def seg_row(block):
    return block[256:272].astype(jnp.float32)[0:1]


def column(row):
    return jnp.transpose(jnp.broadcast_to(row, (128, 128)))


def absorb(q, m, acc, blocks, allowed):
    keys = jnp.concatenate([b[0:128] for b in blocks], 0)
    values = jnp.concatenate([b[128:256] for b in blocks], 1)
    s = lax.dot_general(keys, q, (((1,), (1,)), ((), ())), preferred_element_type=jnp.float32)
    allowed = jnp.concatenate(allowed, 0)
    s = jnp.concatenate(
        [jnp.where(allowed, s[:, h : h + 128], NEG) for h in range(0, s.shape[1], 128)], 1
    )
    top = jnp.max(s, axis=0, keepdims=True)
    new_m = top if m is None else jnp.maximum(m, top)
    weight = jnp.exp2((s - new_m) * SCALE).astype(jnp.bfloat16)
    ones = jnp.ones((ACC_ROWS - 128, values.shape[1]), values.dtype)
    part = jnp.dot(
        jnp.concatenate([values, ones], 0), weight, preferred_element_type=jnp.float32
    )
    if m is not None:
        part = acc * jnp.exp2((m - new_m) * SCALE) + part
    return new_m, part


def pack_kernel(k_ref, v_ref, seg_ref, out_ref, v_buf, seg_buf, sems):
    copies = [
        pltpu.make_async_copy(k_ref, out_ref.at[0, 0:128, :], sems.at[0]),
        pltpu.make_async_copy(v_ref, v_buf, sems.at[1]),
        pltpu.make_async_copy(seg_ref, seg_buf, sems.at[2]),
    ]
    for copy in copies:
        copy.start()
    for copy in copies:
        copy.wait()
    out_ref[0, 128:256, :] = jnp.transpose(v_buf[...].astype(jnp.float32)).astype(out_ref.dtype)
    seg = (seg_buf[...] + 1).astype(jnp.float32)
    out_ref[0, 256:272, :] = jnp.broadcast_to(seg, (16, 128)).astype(out_ref.dtype)


def own_kernel(q_ref, own_ref, m_ref, acc_ref, heads_ref):
    width = q_ref.shape[1]
    q = jnp.concatenate(
        [q_ref[:, h * HEAD_DIM : (h + 1) * HEAD_DIM] for h in range(width // HEAD_DIM)], 0
    )
    heads_ref[...] = q
    own = own_ref[0]
    seg = seg_row(own)
    later = lax.broadcasted_iota(jnp.int32, (128, 128), 0) > lax.broadcasted_iota(
        jnp.int32, (128, 128), 1
    )
    allowed = (column(seg) == seg) & ~later
    m, acc = absorb(q, None, None, [own], [allowed])
    m_ref[...] = jnp.broadcast_to(m, m_ref.shape)
    acc_ref[...] = acc


def gather_blocks(refs):
    return [ref[(*lead,)] for ref in refs for lead in _leads(ref.shape[:-2])]


def _leads(shape):
    if not shape:
        return [()]
    return [(i, *rest) for i in range(shape[0]) for rest in _leads(shape[1:])]


def run(q_ref, own_ref, m_in, acc_in, refs):
    blocks = gather_blocks(refs)
    seg = seg_row(own_ref[0])
    allowed = [column(seg_row(block)) == seg for block in blocks]
    return absorb(q_ref[...], m_in[0:1], acc_in[...], blocks, allowed)


def group_kernel(q_ref, own_ref, m_in, acc_in, *rest):
    *refs, m_ref, acc_ref = rest
    m, acc = run(q_ref, own_ref, m_in, acc_in, refs)
    m_ref[...] = jnp.broadcast_to(m, m_ref.shape)
    acc_ref[...] = acc


def last_kernel(q_ref, own_ref, m_in, acc_in, far_ref, beyond_ref, att_ref):
    _, acc = run(q_ref, own_ref, m_in, acc_in, [far_ref, beyond_ref])
    result = acc[0:128] / acc[128:129]
    for h in range(q_ref.shape[0] // att_ref.shape[0]):
        part = slice(h * HEAD_DIM, (h + 1) * HEAD_DIM)
        att_ref[:, part] = jnp.transpose(result[:, part]).astype(att_ref.dtype)


def project_kernel(steps, lane_ref, att_ref, w_ref, *outs):
    for k, ref in zip(steps, outs):
        width = ref.shape[1]
        columns = pl.ds(pl.multiple_of((lane_ref[0] ^ k) * width, width), width)
        ref[...] = jnp.dot(
            att_ref[...], w_ref[:, columns], preferred_element_type=jnp.float32
        ).astype(ref.dtype)


def on_device(size, queries, keys, values, segment_ids, out_weight):
    tokens = queries.shape[0]
    rows = tokens * (queries.shape[1] // HEAD_DIM)
    index = lax.axis_index("ctx")
    lane = lax.axis_index("tp")
    z, x, c = index // 8, index % 8 // 2, index % 2

    def send(value, pairs):
        return lax.ppermute(value, "ctx", pairs)

    own = pl.pallas_call(
        pack_kernel,
        out_shape=jax.ShapeDtypeStruct((1, 272, 128), jnp.bfloat16),
        in_specs=[HBM] * 3,
        out_specs=VMEM,
        scratch_shapes=[
            pltpu.VMEM((128, 128), jnp.bfloat16),
            pltpu.VMEM((1, 128), jnp.int32),
            pltpu.SemaphoreType.DMA((3,)),
        ],
        compiler_params=params(60),
        name="pack",
    )(keys, values, segment_ids[None])

    state_shape = (
        jax.ShapeDtypeStruct((8, rows), jnp.float32),
        jax.ShapeDtypeStruct((ACC_ROWS, rows), jnp.float32),
    )

    def attend(name, state, blocks, operands):
        return pl.pallas_call(
            group_kernel,
            out_shape=state_shape,
            in_specs=[VMEM] * (4 + len(operands)),
            out_specs=(VMEM, VMEM),
            compiler_params=params(16),
            cost_estimate=cost(blocks, rows),
            name=name,
        )(heads, own, *state, *operands)

    p1 = send(own, shift_z(size, 1))
    p2 = send(own, shift_z(size, 2))
    *state, heads = pl.pallas_call(
        own_kernel,
        out_shape=(*state_shape, jax.ShapeDtypeStruct((rows, HEAD_DIM), queries.dtype)),
        in_specs=[VMEM] * 2,
        out_specs=(VMEM,) * 3,
        compiler_params=params(12),
        cost_estimate=cost(1, rows),
        name="own",
    )(queries, own)
    p1, p2, state, heads = lax.optimization_barrier((p1, p2, state, heads))
    p12 = jnp.concatenate([p1, p2], 0)

    near_a = [p12] + [send(p12, shift_x(size, k)) for k in (2, 1, 3)]
    onward = z < size // 8 - 2
    p12_on = jnp.concatenate(
        [jnp.where(onward & (z >= 1), p1, 0), jnp.where(onward & (z >= 2), p2, 0)], 0
    )
    p34 = send(p12_on, shift_z(size, 2))
    near_a[2], near_a[3], near_a[1], p34, near_a[0] = lax.optimization_barrier(
        (near_a[2], near_a[3], near_a[1], p34, near_a[0])
    )

    def with_either(first):
        return jnp.concatenate([p34[0:1], jnp.where(first, own, p34[1:2])], 0)

    side_b = [send(with_either(x + k < 4), shift_x(size, k)) for k in (2, 1, 3)]
    beyond = send(p34[1:2], [(i, i + 1) for i in range(32, size - 1)])
    far_a = send(jnp.stack(near_a), swap_core(size))
    state = attend("near_a", state, 8, near_a)
    state = attend("far_a", state, 10, [far_a, p34])
    side_b[1], side_b[2], side_b[0], beyond, state = lax.optimization_barrier(
        (side_b[1], side_b[2], side_b[0], beyond, state)
    )

    far_b = send(jnp.stack([with_either(c == 0), *side_b]), swap_core(size))
    state = attend("near_b", state, 6, side_b)
    attention = pl.pallas_call(
        last_kernel,
        out_shape=jax.ShapeDtypeStruct(queries.shape, queries.dtype),
        in_specs=[VMEM] * 6,
        out_specs=VMEM,
        compiler_params=params(16),
        cost_estimate=cost(9, rows),
        name="last",
    )(heads, own, *state, far_b, beyond)

    width = out_weight.shape[1] // 4

    def project(name, steps, dtypes, weigh=1):
        return pl.pallas_call(
            functools.partial(project_kernel, steps),
            out_shape=tuple(jax.ShapeDtypeStruct((tokens, width), dtype) for dtype in dtypes),
            in_specs=[SMEM] + [VMEM] * 2,
            out_specs=(VMEM,) * len(steps),
            compiler_params=params(8),
            cost_estimate=pl.CostEstimate(
                flops=weigh * 2 * len(steps) * tokens * width * out_weight.shape[0],
                bytes_accessed=2 * len(steps) * width * out_weight.shape[0],
                transcendentals=0,
            ),
            name=name,
        )(lane[None], attention, out_weight)

    def pass_on(part, k):
        return lax.ppermute(part, "tp", [(i, i ^ k) for i in range(4)])

    (share_2,) = project("project_2", (2,), [jnp.bfloat16])
    got_2 = pass_on(share_2, 2)
    _, attention = lax.optimization_barrier((share_2, attention))
    share_1, share_3 = project("project_1_3", (1, 3), [jnp.bfloat16] * 2, 64)
    (total,) = project("project_own", (0,), (jnp.float32,), 64)
    for got in (got_2, pass_on(share_1, 1), pass_on(share_3, 3)):
        total = total + got.astype(jnp.float32)
    return total.astype(jnp.bfloat16)


def solution(mesh):
    placed = (P("ctx", "tp"), P("ctx", "tp"), P("ctx", "tp"), P("ctx"), P("tp", None))
    return jax.shard_map(
        functools.partial(on_device, mesh.shape["ctx"]),
        mesh=mesh,
        in_specs=placed,
        out_specs=P("ctx", "tp"),
        check_vma=False,
    )
```
